1024 devices in a mesh: dp: 128 (over y, z_lo, core), mp: 8 (over x, z_hi).
Axes of the slice: x: 4, y: 4, z: 32 (z_hi: 2, z_lo: 16; z = z_hi * 16 + z_lo), core: 2. Of those that a mesh axis runs over, the one named last changes fastest.
Arguments:
- attn: bfloat16 [24576, 3072], P('dp', 'mp'), may hold values from -6 to 6
- w_out: bfloat16 [5120, 3072], P(None, 'mp'), may hold values from -0.109375 to 0.109375
- encoder: bfloat16 [40, 128, 16], replicated, may hold values from -0.5 to 0.5
- decoder: bfloat16 [40, 16, 128], replicated, may hold values from -1.5 to 1.5
- cotangent: bfloat16 [24576, 5120], P('dp'), may hold values from -24 to 24
Outputs:
- mixed: bfloat16 [24576, 5120], P('dp', 'mp')
- grad_attn: bfloat16 [24576, 3072], P('dp', 'mp')
- grad_w: float32 [5120, 3072], P('dp', 'mp')
The draws below stay inside these ranges and needn't reach their ends.
All inputs are finite; a program needn't handle non-finite values.
Results may differ from the reference program's by a relative error of at most 0.0049.
Values sent between devices are 32-bit elements; how exact they have to be, the bound alone decides.
A program may use at most 64 MiB of HBM per device.

```python
import jax
import jax.numpy as jnp
from jax import lax

D = 5120
HD = 128
CODE = 16
HEADS = 24
TOKENS = 24576


def spiked(array, key, source, target, shards_of, factor):
    def block_of(position):
        return (jnp.arange(array.shape[position]) // (array.shape[position] // shards_of)).reshape((-1,) + (1,) * (array.ndim - 1 - position))

    one_side = jax.random.permutation(key, shards_of)[block_of(target)]
    second = (block_of(target) + shards_of // 2) % shards_of
    return jnp.where((block_of(source) == one_side) | (block_of(source) == second), factor * array, array)


def level_of(rng, extent, cuts, least, top_value):
    def one(axis_at, parts):
        heights = jax.random.uniform(jax.random.fold_in(jax.random.fold_in(rng, 6), axis_at), (parts,), jnp.float32, least / len(cuts), top_value / len(cuts))
        return jnp.repeat(jnp.exp(heights), extent[axis_at] // parts).reshape((-1,) + (1,) * (len(extent) - axis_at - 1))

    factor_of = one(*cuts[0])
    for cut in cuts[1:]:
        factor_of = factor_of * one(*cut)
    return factor_of


def centred(key, extent, deviation, bound, shards=(), dtype=jnp.bfloat16):
    loudness = level_of(key, extent, shards, -0.22, 0.18) if shards else 1.0
    values = jax.random.normal(key, extent, jnp.float32) * deviation * loudness
    return jnp.minimum(jnp.maximum(values, -bound), bound).astype(dtype)


def bell_draw_with(key, dims, width, limit, pieces, heavy, dtype=jnp.bfloat16):
    array = width * jax.random.normal(key, dims, jnp.float32)
    if pieces:
        array = array * level_of(key, dims, pieces, -0.22, 0.18)
    return jnp.clip(spiked(array, jax.random.fold_in(key, 3), *heavy), -limit, limit).astype(dtype)


def setup_inputs(seed: int = 0) -> dict:
    splits = jax.random.split(jax.random.key(seed), 6)
    attn = centred(splits[0], (TOKENS, HEADS * HD), 1.0, 6.0, ((0, 128), (1, 8)))
    w_out = centred(splits[1], (D, HEADS * HD), (HEADS * HD) ** -0.5, 0.109375, ((1, 8),))
    encoder = centred(splits[2], (D // HD, HD, CODE), HD ** -0.5, 0.5)
    decoder = centred(splits[3], (D // HD, CODE, HD), CODE ** -0.5, 1.5)
    cotangent = bell_draw_with(splits[4], (TOKENS, D), 1.0, 24.0, ((0, 128),), (0, 1, 128, 5.5))
    return {"attn": attn, "w_out": w_out, "encoder": encoder, "decoder": decoder, "cotangent": cotangent}


def reference(attn, w_out, encoder, decoder, cotangent):
    groups = D // HD
    high = lax.Precision.HIGHEST
    part = jnp.dot(attn, w_out.T, preferred_element_type=jnp.float32)
    code = jnp.einsum("tgh,ghc->tgc", part.reshape(TOKENS, groups, HD), encoder.astype(jnp.float32), precision=high)
    mixed = jnp.einsum("tgc,gch->tgh", code, decoder.astype(jnp.float32), precision=high)
    mixed = mixed.reshape(TOKENS, D).astype(jnp.bfloat16)
    coded = jnp.einsum("tgh,gch->tgc", cotangent.reshape(TOKENS, groups, HD).astype(jnp.float32), decoder.astype(jnp.float32), precision=high)
    spread = jnp.einsum("tgc,ghc->tgh", coded, encoder.astype(jnp.float32), precision=high).reshape(TOKENS, D)
    grad_attn = jnp.dot(spread.astype(jnp.bfloat16), w_out, preferred_element_type=jnp.float32).astype(jnp.bfloat16)
    grad_w = jnp.dot(spread.T, attn.astype(jnp.float32), precision=high) * (float(TOKENS) ** -0.5)
    return mixed, grad_attn, grad_w
```

```python
import functools

import jax
import jax.numpy as jnp
from jax import lax
from jax.experimental import pallas as pl
from jax.experimental.pallas import tpu as pltpu
from jax.sharding import PartitionSpec as P

MESH = pl.DeviceIdType.MESH
F32 = jnp.float32
BF16 = jnp.bfloat16
NN = (((1,), (0,)), ((), ()))
NT = (((1,), (1,)), ((), ()))
TN = (((0,), (0,)), ((), ()))


def dot(a, b, dims):
    return lax.dot_general(a, b, dims, preferred_element_type=F32)


def diagonal(blocks):
    zero = jnp.zeros_like(blocks[0])
    rows = [
        jnp.concatenate([b if i == j else zero for j in range(len(blocks))], axis=1)
        for i, b in enumerate(blocks)
    ]
    return jnp.concatenate(rows, axis=0)


def split(value):
    high = value.astype(BF16).astype(F32)
    return high, value - high


def kernel(
    scale,
    attn_hbm, w_hbm, enc_hbm, dec_hbm, cot_hbm,
    mixed_out, gattn_out, gw_out,
    attn, w, enc, dec, cot,
    w2, chi, clo, term, core_in, y_in, summed, z1_in, quad, z2a_in, z2b_in, pair, whole,
    blk, x_in, zsum, relay_in, far_in, dmain, dtail_a, dtail_b,
    mixed, gattn, gw_rows, gw,
    in_sem, w_sem, cot_sem, out_sem, know8,
    core_s, core_r, y_s, y_r, x_s, x_r, z1_s, z1_r, z2a_s, z2a_r, z2b_s, z2b_r,
    fin_s, fin_r, rel_s, rel_r, far_s, far_r,
):
    dp = lax.axis_index("dp")
    mp = lax.axis_index("mp")
    core = dp % 2
    zl = (dp // 2) % 16
    y = dp // 32
    x = mp // 2
    zh = mp % 2
    z = zh * 16 + zl
    a = zl // 4
    b = zl % 4
    q = a % 2
    half = a // 2
    j = zl % 8

    def along_z(step):
        to = (z + step + 32) % 32
        return ((y * 16 + to % 16) * 2 + core, x * 2 + to // 16)

    other_core = (dp + 1 - 2 * core, mp)
    x_ids = [(dp, ((x + d) % 4) * 2 + zh) for d in (1, 2, 3)]
    y_ids = [((((y + d) % 4) * 16 + zl) * 2 + core, mp) for d in (1, 2, 3)]
    quad_ids = [((y * 16 + a * 4 + (b + d) % 4) * 2 + core, mp) for d in (1, 2, 3)]
    z4_id = ((y * 16 + zl + 4 - 8 * q) * 2 + core, mp)
    z8_id = ((y * 16 + zl + 8 - 16 * half) * 2 + core, mp)

    def remote(src, dst, send, recv, to):
        return pltpu.make_async_remote_copy(
            src_ref=src, dst_ref=dst, send_sem=send, recv_sem=recv,
            device_id=to, device_id_type=MESH,
        )

    barrier = pltpu.get_barrier_semaphore()
    near = [other_core] + x_ids + y_ids + quad_ids + [along_z(4), along_z(-4)]
    for to in near:
        pl.semaphore_signal(barrier, inc=1, device_id=to, device_id_type=MESH)

    attn_copy = pltpu.make_async_copy(attn_hbm, attn, in_sem.at[0])
    dec_copy = pltpu.make_async_copy(dec_hbm, dec, in_sem.at[1])
    enc_copy = pltpu.make_async_copy(enc_hbm, enc, in_sem.at[2])
    dec_copy.start()
    attn_copy.start()
    cot_order = [2 * i + 1 - core for i in range(4)] + [2 * i + core for i in range(4)]
    cot_copies = []
    for i, m in enumerate(cot_order):
        cols = pl.ds(pl.multiple_of(m * 640, 128), 640)
        copy = pltpu.make_async_copy(cot_hbm.at[:, cols], cot.at[i], cot_sem.at[i])
        copy.start()
        cot_copies.append(copy)
    enc_copy.start()
    w_order = [(((x + d) % 4) * 2 + 1 - zh) for d in (1, 2, 3, 0)]
    w_order += [(((x + d) % 4) * 2 + zh) for d in (1, 2, 3, 0)]
    w_copies = []
    for i, m in enumerate(w_order):
        rows = pl.ds(pl.multiple_of(m * 640, 128), 640)
        copy = pltpu.make_async_copy(w_hbm.at[rows, :], w.at[i], w_sem.at[i])
        copy.start()
        w_copies.append(copy)

    dec_copy.wait()
    attn_copy.wait()
    attn_v = attn[...]
    for i, m in enumerate(cot_order):
        cot_copies[i].wait()
        d_block = diagonal([dec[m * 5 + g] for g in range(5)])
        coded = dot(d_block, cot[i], NT)
        high, low = split(coded)
        high = high.astype(BF16)
        chi[m] = high
        clo[m] = low.astype(BF16)
        term[m] = dot(high, attn_v, NN)

    pl.semaphore_wait(barrier, len(near))
    for to in (along_z(4), along_z(-4)):
        pl.semaphore_signal(know8, inc=1, device_id=to, device_id_type=MESH)

    core_copies = []
    for d in (1, 2, 3, 0):
        yy = (y + d) % 4
        copy = remote(
            term.at[2 * yy + 1 - core], core_in.at[yy], core_s.at[d], core_r.at[d], other_core
        )
        copy.start()
        core_copies.append(copy)

    enc_copy.wait()

    def code_blocks(side):
        copies = []
        for i, d in enumerate((1, 2, 3, 0)):
            m = w_order[side * 4 + i]
            w_copies[side * 4 + i].wait()
            e_block = diagonal([enc[m * 5 + g] for g in range(5)])
            w2_block = dot(e_block, w[side * 4 + i], NN).astype(BF16)
            w2[m] = w2_block
            code = dot(w2_block, attn_v, NT)
            to = (x + d) % 4
            blk[side, to, 0:80, :] = code[:, 0:128]
            blk[side, to, 80:120, :] = jnp.concatenate(
                [code[0:40, 128:192], code[40:80, 128:192]], axis=1
            )
            if d:
                copy = remote(
                    blk.at[side, to], x_in.at[side, d - 1],
                    x_s.at[side, d - 1], x_r.at[side, d - 1], x_ids[d - 1],
                )
                copy.start()
                copies.append(copy)
        return copies

    away_copies = code_blocks(0)

    y_copies = []
    for i, d in enumerate((1, 2, 3, 0)):
        yy = (y + d) % 4
        core_copies[i].wait_recv()
        core_in[yy] = core_in[yy] + term[2 * yy + core]
        if d:
            copy = remote(
                core_in.at[yy], y_in.at[d - 1], y_s.at[d - 1], y_r.at[d - 1], y_ids[d - 1]
            )
            copy.start()
            y_copies.append(copy)

    own_copies = code_blocks(1)

    for copy in away_copies:
        copy.wait_recv()
    zsum[...] = blk[0, x] + x_in[0, 0] + x_in[0, 1] + x_in[0, 2]
    pl.semaphore_wait(know8, 2)
    up, down = pl.ds(0, 64), pl.ds(64, 56)
    relays = [
        remote(zsum.at[up], relay_in.at[up], rel_s.at[0], rel_r.at[0], along_z(8)),
        remote(zsum.at[down], relay_in.at[down], rel_s.at[1], rel_r.at[1], along_z(-8)),
    ]
    for copy in relays:
        copy.start()

    for copy in y_copies:
        copy.wait_recv()
    summed[...] = (core_in[y] + y_in[0] + y_in[1] + y_in[2]).reshape(5, 16, 384)

    def needed(at):
        return (at // 2, 2 - at % 2 + at // 2, 3 + at // 2)

    z1_copies = []
    for d in (1, 2, 3):
        for s, group in enumerate(needed((b + d) % 4)):
            copy = remote(
                summed.at[group], z1_in.at[d - 1, s],
                z1_s.at[d - 1, s], z1_r.at[d - 1, s], quad_ids[d - 1],
            )
            copy.start()
            z1_copies.append(copy)

    d_own = diagonal([dec[mp * 5 + g] for g in range(5)]).astype(F32)
    dmain[...] = jnp.concatenate([d_own, d_own], axis=0).astype(BF16)
    dtail_a[...] = jnp.concatenate([d_own[0:40], d_own[0:40]], axis=0).astype(BF16)
    dtail_b[...] = jnp.concatenate([d_own[40:80], d_own[40:80]], axis=0).astype(BF16)

    w2_v = w2[...].reshape(640, 384)
    grad = dot(chi[...].reshape(640, 192), w2_v, TN)
    grad = grad + dot(clo[...].reshape(640, 192), w2_v, TN)
    gattn[...] = grad.astype(BF16)
    gattn_copy = pltpu.make_async_copy(gattn, gattn_out, out_sem.at[0])
    gattn_copy.start()

    for copy in relays:
        copy.wait_recv()
    fars = [
        remote(relay_in.at[up], far_in.at[up], far_s.at[0], far_r.at[0], along_z(8)),
        remote(relay_in.at[down], far_in.at[down], far_s.at[1], far_r.at[1], along_z(-8)),
    ]
    for copy in fars:
        copy.start()

    for copy in z1_copies:
        copy.wait_recv()
    for s, group in enumerate(needed(b)):
        quad[s] = summed[group] + z1_in[0, s] + z1_in[1, s] + z1_in[2, s]
    z2a = remote(quad.at[pl.ds(1 - q, 2)], z2a_in, z2a_s, z2a_r, z4_id)
    z2a.start()

    for copy in own_copies:
        copy.wait_recv()
    code_near = blk[1, x] + x_in[1, 0] + x_in[1, 1] + x_in[1, 2]

    z2a.wait_recv()
    pair[...] = quad[pl.ds(q, 2)] + z2a_in[...]
    z2b = remote(pair, z2b_in, z2b_s, z2b_r, z8_id)
    fin = remote(whole, whole, fin_s, fin_r, other_core)

    @pl.when(half != core)
    def _():
        z2b.start()

    for copy in fars:
        copy.wait_recv()
    code_sum = code_near + far_in[...]
    high, low = split(code_sum)
    main = jnp.concatenate([high[0:80], low[0:80]], axis=0).astype(BF16)
    tail = jnp.concatenate([high[80:120], low[80:120]], axis=0).astype(BF16)
    mixed[0:128, :] = dot(main, dmain[...], TN).astype(BF16)
    tail_a = dot(tail, dtail_a[...], TN)
    tail_b = dot(tail, dtail_b[...], TN)
    mixed[128:192, :] = (tail_a[0:64] + tail_b[64:128]).astype(BF16)
    mixed_copy = pltpu.make_async_copy(mixed, mixed_out, out_sem.at[1])
    mixed_copy.start()

    @pl.when(half == core)
    def _():
        z2b.wait_recv()
        whole[...] = pair[...] + z2b_in[...]
        fin.start()

    @pl.when(half != core)
    def _():
        fin.wait_recv()

    groups = needed(b)
    first = groups[0] * (1 - q) + groups[1] * q
    second = groups[1] * (1 - q) + groups[2] * q
    base = (2 * y + half) * 5
    e_pair = diagonal([enc[base + first], enc[base + second]])
    g_high, g_low = split(whole[...].reshape(32, 384))
    g_both = jnp.concatenate([g_high, g_low], axis=0).astype(BF16)
    e_both = jnp.concatenate([e_pair, e_pair], axis=0)
    gw_rows[...] = dot(e_both, g_both, TN) * scale
    jump = (b % 2) * q
    start = 40 * (2 * j + core) - 128 * (first * (1 - jump) + (second - 1) * jump)
    gw[...] = gw_rows[pl.ds(pl.multiple_of(start, 8), 40), :]
    gw_copy = pltpu.make_async_copy(gw, gw_out, out_sem.at[2])
    gw_copy.start()

    for copy in core_copies + away_copies + y_copies + own_copies + relays + fars + z1_copies:
        copy.wait_send()
    z2a.wait_send()

    @pl.when(half != core)
    def _():
        z2b.wait_send()

    @pl.when(half == core)
    def _():
        fin.wait_send()

    gattn_copy.wait()
    mixed_copy.wait()
    gw_copy.wait()


def solution(mesh):
    dp_count = mesh.shape["dp"]

    def shards(attn, w_out, encoder, decoder, cotangent):
        scale = float(attn.shape[0] * dp_count) ** (-0.5)
        enc_t = jnp.transpose(encoder, (0, 2, 1))
        anywhere = pl.BlockSpec(memory_space=pl.ANY)
        dma = pltpu.SemaphoreType.DMA
        vmem = pltpu.VMEM
        return pl.pallas_call(
            functools.partial(kernel, scale),
            out_shape=(
                jax.ShapeDtypeStruct((192, 640), BF16),
                jax.ShapeDtypeStruct((192, 384), BF16),
                jax.ShapeDtypeStruct((40, 384), F32),
            ),
            in_specs=[anywhere] * 5,
            out_specs=(anywhere,) * 3,
            scratch_shapes=[
                vmem((192, 384), BF16),
                vmem((8, 640, 384), BF16),
                vmem((40, 16, 128), BF16),
                vmem((40, 16, 128), BF16),
                vmem((8, 192, 640), BF16),
                vmem((8, 80, 384), BF16),
                vmem((8, 80, 192), BF16),
                vmem((8, 80, 192), BF16),
                vmem((8, 80, 384), F32),
                vmem((4, 80, 384), F32),
                vmem((3, 80, 384), F32),
                vmem((5, 16, 384), F32),
                vmem((3, 3, 16, 384), F32),
                vmem((3, 16, 384), F32),
                vmem((2, 16, 384), F32),
                vmem((2, 16, 384), F32),
                vmem((2, 16, 384), F32),
                vmem((2, 16, 384), F32),
                vmem((2, 4, 120, 128), F32),
                vmem((2, 3, 120, 128), F32),
                vmem((120, 128), F32),
                vmem((120, 128), F32),
                vmem((120, 128), F32),
                vmem((160, 640), BF16),
                vmem((80, 640), BF16),
                vmem((80, 640), BF16),
                vmem((192, 640), BF16),
                vmem((192, 384), BF16),
                vmem((256, 384), F32),
                vmem((40, 384), F32),
                dma((3,)), dma((8,)), dma((8,)), dma((3,)),
                pltpu.SemaphoreType.REGULAR,
                dma((4,)), dma((4,)),
                dma((3,)), dma((3,)),
                dma((2, 3)), dma((2, 3)),
                dma((3, 3)), dma((3, 3)),
                dma, dma,
                dma, dma,
                dma, dma,
                dma((2,)), dma((2,)),
                dma((2,)), dma((2,)),
            ],
            compiler_params=pltpu.CompilerParams(
                collective_id=0, has_side_effects=True, vmem_limit_bytes=48 * 1024 * 1024
            ),
            name="coded_projection",
        )(attn, w_out, enc_t, decoder, cotangent)

    return jax.shard_map(
        shards,
        mesh=mesh,
        in_specs=(P("dp", "mp"), P(None, "mp"), P(), P(), P("dp", None)),
        out_specs=(P("dp", "mp"), P("dp", "mp"), P("dp", "mp")),
        check_vma=False,
    )
```

```python
import functools

import jax
import jax.numpy as jnp
from jax import lax
from jax.experimental import pallas as pl
from jax.experimental.pallas import tpu as pltpu
from jax.sharding import PartitionSpec as P

MESH = pl.DeviceIdType.MESH
CUTS = 3
F32 = jnp.float32
BF16 = jnp.bfloat16
NN = (((1,), (0,)), ((), ()))
NT = (((1,), (1,)), ((), ()))
TN = (((0,), (0,)), ((), ()))


def dot(a, b, dims):
    return lax.dot_general(a, b, dims, preferred_element_type=F32)


def diagonal(blocks):
    zero = jnp.zeros_like(blocks[0])
    rows = [
        jnp.concatenate([b if i == j else zero for j in range(len(blocks))], axis=1)
        for i, b in enumerate(blocks)
    ]
    return jnp.concatenate(rows, axis=0)


def split(value):
    high = value.astype(BF16).astype(F32)
    return high, value - high


def kernel(
    scale,
    attn_hbm, w_hbm, enc_hbm, dec_hbm, cot_hbm,
    mixed_out, gattn_out, gw_out,
    attn, w, enc, dec, cot,
    w2, chi, clo, term, core_in, y_in, classes, z1_in, quad, z2a_in, z2b_in, pair, whole,
    blk, x_in, zsum, relay_in, far_in, dmain, dtail_a, dtail_b, gw_rows,
    in_sem, w_sem, cot_sem, ready8, ready16,
    core_s, core_r, y_s, y_r, x_s, x_r, z1_s, z1_r, z2a_s, z2a_r, z2b_s, z2b_r,
    fin_s, fin_r, far_s, far_r, rel_s, rel_r,
):
    dp = lax.axis_index("dp")
    mp = lax.axis_index("mp")
    core = dp % 2
    zl = (dp // 2) % 16
    y = dp // 32
    x = mp // 2
    zh = mp % 2
    a = zl // 4
    b = zl % 4
    q = a % 2
    half = a // 2
    j = zl % 8

    other_core = (dp + 1 - 2 * core, mp)
    x_ids = [(dp, ((x + d) % 4) * 2 + zh) for d in (1, 2, 3)]
    y_ids = [((((y + d) % 4) * 16 + zl) * 2 + core, mp) for d in (1, 2, 3)]
    quad_ids = [((y * 16 + a * 4 + (b + d) % 4) * 2 + core, mp) for d in (1, 2, 3)]
    z4_id = ((y * 16 + zl + 4 - 8 * q) * 2 + core, mp)
    z8_id = ((y * 16 + zl + 8 - 16 * half) * 2 + core, mp)

    def remote(src, dst, send, recv, to):
        return pltpu.make_async_remote_copy(
            src_ref=src, dst_ref=dst, send_sem=send, recv_sem=recv,
            device_id=to, device_id_type=MESH,
        )

    barrier = pltpu.get_barrier_semaphore()
    near = [other_core] + x_ids + y_ids + quad_ids + [z4_id]
    z16_id = ((y * 16 + a * 4 + (b + 2) % 4) * 2 + core, x * 2 + 1 - zh)
    for to in near:
        pl.semaphore_signal(barrier, inc=1, device_id=to, device_id_type=MESH)

    @pl.when(half == 0)
    def _():
        pl.semaphore_signal(barrier, inc=1, device_id=z8_id, device_id_type=MESH)

    @pl.when(zh == 0)
    def _():
        pl.semaphore_signal(barrier, inc=1, device_id=z16_id, device_id_type=MESH)

    attn_copy = pltpu.make_async_copy(attn_hbm, attn, in_sem.at[0])
    dec_copy = pltpu.make_async_copy(dec_hbm, dec, in_sem.at[1])
    enc_copy = pltpu.make_async_copy(enc_hbm, enc, in_sem.at[2])
    dec_copy.start()
    attn_copy.start()
    cot_order = [2 * i + 1 - core for i in range(4)] + [2 * i + core for i in range(4)]
    cot_copies = []
    for i, m in enumerate(cot_order):
        cols = pl.ds(pl.multiple_of(m * 640, 128), 640)
        copy = pltpu.make_async_copy(cot_hbm.at[:, cols], cot.at[i], cot_sem.at[i])
        copy.start()
        cot_copies.append(copy)
    enc_copy.start()
    w_order = [(((x + d) % 4) * 2 + 1 - zh) for d in (1, 2, 3, 0)]
    w_order += [(((x + d) % 4) * 2 + zh) for d in (1, 2, 3, 0)]
    w_copies = []
    for i, m in enumerate(w_order):
        rows = pl.ds(pl.multiple_of(m * 640, 128), 640)
        copy = pltpu.make_async_copy(w_hbm.at[rows, :], w.at[i], w_sem.at[i])
        copy.start()
        w_copies.append(copy)

    dec_copy.wait()
    attn_copy.wait()
    attn_v = attn[...]

    wide = 384 // CUTS

    def gradient_terms(side):
        for i in range(4):
            cot_copies[4 * side + i].wait()
        for i in range(4 * side, 4 * side + 4):
            m = cot_order[i]
            d_block = diagonal([dec[m * 5 + g] for g in range(5)])
            coded = dot(d_block, cot[i], NT)
            high, low = split(coded)
            high = high.astype(BF16)
            chi[m] = high
            clo[m] = low.astype(BF16)
            product = dot(high, attn_v, NN)
            for l in range(CUTS):
                term[l, m % 2, m // 2] = product[:, wide * l:wide * (l + 1)]

    gradient_terms(0)
    pl.semaphore_wait(barrier, len(near) + half + zh)
    core_copies = []
    for l in range(CUTS):
        copy = remote(
            term.at[l, 1 - core], core_in.at[l], core_s.at[l], core_r.at[l], other_core
        )
        copy.start()
        core_copies.append(copy)

    @pl.when(half == 1)
    def _():
        pl.semaphore_signal(ready8, inc=1, device_id=z8_id, device_id_type=MESH)

    @pl.when(zh == 1)
    def _():
        pl.semaphore_signal(ready16, inc=1, device_id=z16_id, device_id_type=MESH)

    enc_copy.wait()

    def code_blocks(side):
        for i in range(4):
            w_copies[4 * side + i].wait()
        for i in range(4):
            m = w_order[4 * side + i]
            to = m // 2
            e_block = diagonal([enc[m * 5 + g] for g in range(5)])
            w2_block = dot(e_block, w[4 * side + i], NN).astype(BF16)
            w2[m] = w2_block
            code = dot(w2_block, attn_v, NT)
            blk[side, to, 0:80, :] = code[:, 0:128]
            blk[side, to, 80:120, :] = jnp.concatenate(
                [code[0:40, 128:192], code[40:80, 128:192]], axis=1
            )
        copies = []
        for d in (1, 2, 3):
            copy = remote(
                blk.at[side, (x + d) % 4], x_in.at[side, d - 1],
                x_s.at[side, d - 1], x_r.at[side, d - 1], x_ids[d - 1],
            )
            copy.start()
            copies.append(copy)
        return copies

    away_copies = code_blocks(0)
    gradient_terms(1)

    far = remote(zsum, relay_in, far_s, far_r, z16_id)
    last = remote(relay_in, far_in, rel_s, rel_r, quad_ids[1])

    def send_away():
        for copy in away_copies:
            copy.wait_recv()
        zsum[...] = blk[0, x] + x_in[0, 0] + x_in[0, 1] + x_in[0, 2]
        far.start()

    @pl.when(zh == 1)
    def _():
        send_away()

    y_copies = [[] for _ in range(CUTS)]
    for l in range(CUTS):
        core_copies[l].wait_recv()
        for d in (1, 2, 3, 0):
            yy = (y + d) % 4
            core_in[l, yy] = core_in[l, yy] + term[l, core, yy]
            if d:
                copy = remote(
                    core_in.at[l, yy], y_in.at[l, d - 1],
                    y_s.at[l, d - 1], y_r.at[l, d - 1], y_ids[d - 1],
                )
                copy.start()
                y_copies[l].append(copy)

    own_copies = code_blocks(1)

    def needed(at):
        return (at // 2, 2 - at % 2 + at // 2, 3 + at // 2)

    z1_copies = [[] for _ in range(CUTS)]
    for l in range(CUTS):
        for copy in y_copies[l]:
            copy.wait_recv()
        total = core_in[l, y] + y_in[l, 0] + y_in[l, 1] + y_in[l, 2]
        total = total.reshape(5, 16, wide)
        for at in range(4):
            for s, group in enumerate(needed(at)):
                classes[l, at, s] = total[group]
        for d in (1, 2, 3):
            copy = remote(
                classes.at[l, (b + d) % 4], z1_in.at[l, d - 1],
                z1_s.at[l, d - 1], z1_r.at[l, d - 1], quad_ids[d - 1],
            )
            copy.start()
            z1_copies[l].append(copy)

    d_own = diagonal([dec[mp * 5 + g] for g in range(5)]).astype(F32)
    dmain[...] = jnp.concatenate([d_own, d_own], axis=0).astype(BF16)
    dtail_a[...] = jnp.concatenate([d_own[0:40], d_own[0:40]], axis=0).astype(BF16)
    dtail_b[...] = jnp.concatenate([d_own[40:80], d_own[40:80]], axis=0).astype(BF16)

    w2_v = w2[...].reshape(640, 384)
    grad = dot(chi[...].reshape(640, 192), w2_v, TN)
    grad = grad + dot(clo[...].reshape(640, 192), w2_v, TN)
    gattn_out[...] = grad.astype(BF16)

    single = b % 2 == q
    z2a_copies = []
    for l in range(CUTS):
        for copy in z1_copies[l]:
            copy.wait_recv()
        quad[l] = classes[l, b] + z1_in[l, 0] + z1_in[l, 1] + z1_in[l, 2]
        two = remote(
            quad.at[l, pl.ds(1 - q, 2)], z2a_in.at[l], z2a_s.at[l], z2a_r.at[l], z4_id
        )
        one = remote(
            quad.at[l, pl.ds(2 - 2 * q, 1)], z2a_in.at[l, pl.ds(1 - q, 1)],
            z2a_s.at[l], z2a_r.at[l], z4_id,
        )
        z2a_copies.append((one, two))

        @pl.when(single)
        def _(two=two):
            two.start()

        @pl.when(jnp.logical_not(single))
        def _(one=one):
            one.start()

    for copy in own_copies:
        copy.wait_recv()
    code_near = blk[1, x] + x_in[1, 0] + x_in[1, 1] + x_in[1, 2]

    @pl.when(half == 0)
    def _():
        pl.semaphore_wait(ready8, 1)

    z2b_copies = [
        (
            remote(
                pair.at[l, pl.ds(q, 1)], z2b_in.at[l, pl.ds(q, 1)],
                z2b_s.at[l], z2b_r.at[l], z8_id,
            ),
            remote(pair.at[l], z2b_in.at[l], z2b_s.at[l], z2b_r.at[l], z8_id),
        )
        for l in range(CUTS)
    ]
    fin_copies = [
        remote(whole.at[l], whole.at[l], fin_s.at[l], fin_r.at[l], other_core) for l in range(CUTS)
    ]
    for l in range(CUTS):
        pair[l] = quad[l, pl.ds(q, 2)]

        @pl.when(single)
        def _(l=l):
            z2a_copies[l][0].wait_recv()
            pair[l, q] = pair[l, q] + z2a_in[l, q]

            @pl.when(half != core)
            def _():
                z2b_copies[l][0].start()

        @pl.when(jnp.logical_not(single))
        def _(l=l):
            z2a_copies[l][1].wait_recv()
            pair[l] = pair[l] + z2a_in[l]

            @pl.when(half != core)
            def _():
                z2b_copies[l][1].start()

    @pl.when(zh == 0)
    def _():
        pl.semaphore_wait(ready16, 1)
        send_away()

    far.wait_recv()
    last.start()

    @pl.when(half == core)
    def _():
        for l in range(CUTS):
            whole[l] = pair[l]

            @pl.when(single)
            def _(l=l):
                z2b_copies[l][0].wait_recv()
                whole[l, q] = whole[l, q] + z2b_in[l, q]

            @pl.when(jnp.logical_not(single))
            def _(l=l):
                z2b_copies[l][1].wait_recv()
                whole[l] = whole[l] + z2b_in[l]

            fin_copies[l].start()

    last.wait_recv()
    code_sum = code_near + far_in[...]
    high, low = split(code_sum)
    main = jnp.concatenate([high[0:80], low[0:80]], axis=0).astype(BF16)
    tail = jnp.concatenate([high[80:120], low[80:120]], axis=0).astype(BF16)
    mixed_out[0:128, :] = dot(main, dmain[...], TN).astype(BF16)
    tail_a = dot(tail, dtail_a[...], TN)
    tail_b = dot(tail, dtail_b[...], TN)
    mixed_out[128:192, :] = (tail_a[0:64] + tail_b[64:128]).astype(BF16)

    groups = needed(b)
    first = groups[0] * (1 - q) + groups[1] * q
    second = groups[1] * (1 - q) + groups[2] * q
    base = (2 * y + half) * 5
    e_pair = diagonal([enc[base + first], enc[base + second]])
    e_both = jnp.concatenate([e_pair, e_pair], axis=0)

    @pl.when(half != core)
    def _():
        for l in range(CUTS):
            fin_copies[l].wait_recv()

    for l in range(CUTS):
        g_high, g_low = split(whole[l].reshape(32, wide))
        g_both = jnp.concatenate([g_high, g_low], axis=0).astype(BF16)
        gw_rows[:, wide * l:wide * (l + 1)] = dot(e_both, g_both, TN) * scale
    jump = (b % 2) * q
    start = 40 * (2 * j + core) - 128 * (first * (1 - jump) + (second - 1) * jump)
    gw_out[...] = gw_rows[pl.ds(pl.multiple_of(start, 8), 40), :]

    for copy in core_copies + away_copies + own_copies + [far, last]:
        copy.wait_send()
    for l in range(CUTS):
        for copy in y_copies[l] + z1_copies[l]:
            copy.wait_send()

    for pick, want in ((0, single), (1, jnp.logical_not(single))):
        @pl.when(want)
        def _(pick=pick):
            for l in range(CUTS):
                z2a_copies[l][1 - pick].wait_send()

                @pl.when(half != core)
                def _(l=l):
                    z2b_copies[l][pick].wait_send()

    @pl.when(half == core)
    def _():
        for l in range(CUTS):
            fin_copies[l].wait_send()


def finish(mixed, gattn, gw, mixed_out, gattn_out, gw_out, sem):
    copies = [
        pltpu.make_async_copy(mixed, mixed_out, sem.at[0]),
        pltpu.make_async_copy(gattn, gattn_out, sem.at[1]),
        pltpu.make_async_copy(gw, gw_out, sem.at[2]),
    ]
    for copy in copies:
        copy.start()
    for copy in copies:
        copy.wait()


def solution(mesh):
    dp_count = mesh.shape["dp"]

    def shards(attn, w_out, encoder, decoder, cotangent):
        scale = float(attn.shape[0] * dp_count) ** (-0.5)
        enc_t = jnp.transpose(encoder, (0, 2, 1))
        wide = 384 // CUTS
        hbm = pl.BlockSpec(memory_space=pltpu.HBM)
        near = pl.BlockSpec(memory_space=pltpu.VMEM)
        shapes = (
            jax.ShapeDtypeStruct((192, 640), BF16),
            jax.ShapeDtypeStruct((192, 384), BF16),
            jax.ShapeDtypeStruct((40, 384), F32),
        )
        dma = pltpu.SemaphoreType.DMA
        vmem = pltpu.VMEM
        results = pl.pallas_call(
            functools.partial(kernel, scale),
            out_shape=shapes,
            in_specs=[hbm] * 5,
            out_specs=(near,) * 3,
            scratch_shapes=[
                vmem((192, 384), BF16),
                vmem((8, 640, 384), BF16),
                vmem((40, 16, 128), BF16),
                vmem((40, 16, 128), BF16),
                vmem((8, 192, 640), BF16),
                vmem((8, 80, 384), BF16),
                vmem((8, 80, 192), BF16),
                vmem((8, 80, 192), BF16),
                vmem((CUTS, 2, 4, 80, wide), F32),
                vmem((CUTS, 4, 80, wide), F32),
                vmem((CUTS, 3, 80, wide), F32),
                vmem((CUTS, 4, 3, 16, wide), F32),
                vmem((CUTS, 3, 3, 16, wide), F32),
                vmem((CUTS, 3, 16, wide), F32),
                vmem((CUTS, 2, 16, wide), F32),
                vmem((CUTS, 2, 16, wide), F32),
                vmem((CUTS, 2, 16, wide), F32),
                vmem((CUTS, 2, 16, wide), F32),
                vmem((2, 4, 120, 128), F32),
                vmem((2, 3, 120, 128), F32),
                vmem((120, 128), F32),
                vmem((120, 128), F32),
                vmem((120, 128), F32),
                vmem((160, 640), BF16),
                vmem((80, 640), BF16),
                vmem((80, 640), BF16),
                vmem((256, 384), F32),
                dma((3,)), dma((8,)), dma((8,)),
                pltpu.SemaphoreType.REGULAR, pltpu.SemaphoreType.REGULAR,
                dma((3,)), dma((3,)),
                dma((3, 3)), dma((3, 3)),
                dma((2, 3)), dma((2, 3)),
                dma((3, 3)), dma((3, 3)),
                dma((3,)), dma((3,)),
                dma((3,)), dma((3,)),
                dma((3,)), dma((3,)),
                dma, dma,
                dma, dma,
            ],
            compiler_params=pltpu.CompilerParams(
                collective_id=0, has_side_effects=True, vmem_limit_bytes=56 * 1024 * 1024
            ),
            name="coded_projection",
        )(attn, w_out, enc_t, decoder, cotangent)
        return pl.pallas_call(
            finish,
            out_shape=shapes,
            in_specs=[near] * 3,
            out_specs=(hbm,) * 3,
            scratch_shapes=[dma((3,))],
            name="finish",
        )(*results)

    return jax.shard_map(
        shards,
        mesh=mesh,
        in_specs=(P("dp", "mp"), P(None, "mp"), P(), P(), P("dp", None)),
        out_specs=(P("dp", "mp"), P("dp", "mp"), P("dp", "mp")),
        check_vma=False,
    )
```

```python
import functools

import jax
import jax.numpy as jnp
from jax import lax
from jax.experimental import pallas as pl
from jax.experimental.pallas import tpu as pltpu
from jax.sharding import PartitionSpec as P

MESH = pl.DeviceIdType.MESH
CUTS = 3
F32 = jnp.float32
BF16 = jnp.bfloat16
NN = (((1,), (0,)), ((), ()))
NT = (((1,), (1,)), ((), ()))
TN = (((0,), (0,)), ((), ()))


def dot(a, b, dims):
    return lax.dot_general(a, b, dims, preferred_element_type=F32)


def diagonal(blocks):
    zero = jnp.zeros_like(blocks[0])
    rows = [
        jnp.concatenate([b if i == j else zero for j in range(len(blocks))], axis=1)
        for i, b in enumerate(blocks)
    ]
    return jnp.concatenate(rows, axis=0)


def split(value):
    high = value.astype(BF16).astype(F32)
    return high, value - high


def kernel(
    scale,
    attn_hbm, w_hbm, enc_hbm, dec_hbm, cot_hbm,
    mixed_out, gattn_out, gw_out,
    attn, w, enc, dec, cot,
    w2, chi, clo, term, core_in, y_in, classes, z1_in, quad, z2a_in, z2b_in, pair, whole,
    blk, x_in, zsum, relay_in, far_in, dmain, dtail_a, dtail_b, gw_rows,
    in_sem, w_sem, cot_sem, ready8, ready16,
    core_s, core_r, y_s, y_r, x_s, x_r, z1_s, z1_r, z2a_s, z2a_r, z2b_s, z2b_r,
    fin_s, fin_r, far_s, far_r, rel_s, rel_r,
):
    dp = lax.axis_index("dp")
    mp = lax.axis_index("mp")
    core = dp % 2
    zl = (dp // 2) % 16
    y = dp // 32
    x = mp // 2
    zh = mp % 2
    a = zl // 4
    b = zl % 4
    q = a % 2
    half = a // 2
    j = zl % 8

    other_core = (dp + 1 - 2 * core, mp)
    x_ids = [(dp, ((x + d) % 4) * 2 + zh) for d in (1, 2, 3)]
    y_ids = [((((y + d) % 4) * 16 + zl) * 2 + core, mp) for d in (1, 2, 3)]
    quad_ids = [((y * 16 + a * 4 + (b + d) % 4) * 2 + core, mp) for d in (1, 2, 3)]
    z4_id = ((y * 16 + zl + 4 - 8 * q) * 2 + core, mp)
    z8_id = ((y * 16 + zl + 8 - 16 * half) * 2 + core, mp)

    def remote(src, dst, send, recv, to):
        return pltpu.make_async_remote_copy(
            src_ref=src, dst_ref=dst, send_sem=send, recv_sem=recv,
            device_id=to, device_id_type=MESH,
        )

    barrier = pltpu.get_barrier_semaphore()
    near = [other_core] + x_ids + y_ids + quad_ids + [z4_id]
    z16_id = ((y * 16 + a * 4 + (b + 2) % 4) * 2 + core, x * 2 + 1 - zh)
    for to in near:
        pl.semaphore_signal(barrier, inc=1, device_id=to, device_id_type=MESH)

    @pl.when(half == 0)
    def _():
        pl.semaphore_signal(barrier, inc=1, device_id=z8_id, device_id_type=MESH)

    @pl.when(zh == 0)
    def _():
        pl.semaphore_signal(barrier, inc=1, device_id=z16_id, device_id_type=MESH)

    attn_copy = pltpu.make_async_copy(attn_hbm, attn, in_sem.at[0])
    dec_copy = pltpu.make_async_copy(dec_hbm, dec, in_sem.at[1])
    enc_copy = pltpu.make_async_copy(enc_hbm, enc, in_sem.at[2])
    dec_copy.start()
    attn_copy.start()
    cot_order = [2 * i + 1 - core for i in range(4)] + [2 * i + core for i in range(4)]
    cot_copies = []
    for i, m in enumerate(cot_order):
        cols = pl.ds(pl.multiple_of(m * 640, 128), 640)
        cot_copies.append(pltpu.make_async_copy(cot_hbm.at[:, cols], cot.at[i], cot_sem.at[i]))
    w_order = [(((x + d) % 4) * 2 + 1 - zh) for d in (1, 2, 3, 0)]
    w_order += [(((x + d) % 4) * 2 + zh) for d in (1, 2, 3, 0)]
    w_copies = []
    for i, m in enumerate(w_order):
        rows = pl.ds(pl.multiple_of(m * 640, 128), 640)
        w_copies.append(pltpu.make_async_copy(w_hbm.at[rows, :], w.at[i], w_sem.at[i]))

    enc_copy.start()

    @pl.when(zh == 0)
    def _():
        for copy in cot_copies + w_copies:
            copy.start()

    @pl.when(zh == 1)
    def _():
        for copy in w_copies[:4] + cot_copies + w_copies[4:]:
            copy.start()

    dec_copy.wait()
    attn_copy.wait()

    wide = 384 // CUTS

    def gradient_terms(side):
        for i in range(4):
            cot_copies[4 * side + i].wait()
        for i in range(4 * side, 4 * side + 4):
            m = cot_order[i]
            d_block = diagonal([dec[m * 5 + g] for g in range(5)])
            coded = dot(d_block, cot[i], NT)
            high, low = split(coded)
            high = high.astype(BF16)
            chi[m] = high
            clo[m] = low.astype(BF16)
            product = dot(high, attn[...], NN)
            for l in range(CUTS):
                term[l, m % 2, m // 2] = product[:, wide * l:wide * (l + 1)]

    def code_blocks(side):
        for i in range(4):
            w_copies[4 * side + i].wait()
        for i in range(4):
            m = w_order[4 * side + i]
            to = m // 2
            e_block = diagonal([enc[m * 5 + g] for g in range(5)])
            w2_block = dot(e_block, w[4 * side + i], NN).astype(BF16)
            w2[m] = w2_block
            code = dot(w2_block, attn[...], NT)
            blk[side, to, 0:80, :] = code[:, 0:128]
            blk[side, to, 80:120, :] = jnp.concatenate(
                [code[0:40, 128:192], code[40:80, 128:192]], axis=1
            )

    away_copies, own_copies = [
        [
            remote(
                blk.at[side, (x + d) % 4], x_in.at[side, d - 1],
                x_s.at[side, d - 1], x_r.at[side, d - 1], x_ids[d - 1],
            )
            for d in (1, 2, 3)
        ]
        for side in (0, 1)
    ]

    enc_copy.wait()

    @pl.when(zh == 0)
    def _():
        gradient_terms(0)

    @pl.when(zh == 1)
    def _():
        code_blocks(0)

    pl.semaphore_wait(barrier, len(near) + half + zh)

    @pl.when(zh == 1)
    def _():
        for copy in away_copies:
            copy.start()
        gradient_terms(0)

    core_copies = []
    for l in range(CUTS):
        copy = remote(
            term.at[l, 1 - core], core_in.at[l], core_s.at[l], core_r.at[l], other_core
        )
        copy.start()
        core_copies.append(copy)

    @pl.when(half == 1)
    def _():
        pl.semaphore_signal(ready8, inc=1, device_id=z8_id, device_id_type=MESH)

    @pl.when(zh == 1)
    def _():
        pl.semaphore_signal(ready16, inc=1, device_id=z16_id, device_id_type=MESH)

    gradient_terms(1)

    pieces = [pl.ds(0, 32), pl.ds(32, 32), pl.ds(64, 32), pl.ds(96, 24)]
    fars = [
        remote(zsum.at[piece], relay_in.at[piece], far_s.at[i], far_r.at[i], z16_id)
        for i, piece in enumerate(pieces)
    ]
    last = remote(relay_in, far_in, rel_s, rel_r, quad_ids[1])

    def send_away():
        for copy in away_copies:
            copy.wait_recv()
        zsum[...] = blk[0, x] + x_in[0, 0] + x_in[0, 1] + x_in[0, 2]
        fars[0].start()

    @pl.when(zh == 1)
    def _():
        send_away()

    y_copies = [[] for _ in range(CUTS)]
    for l in range(CUTS):
        core_copies[l].wait_recv()
        for d in (1, 2, 3, 0):
            yy = (y + d) % 4
            core_in[l, yy] = core_in[l, yy] + term[l, core, yy]
            if d:
                copy = remote(
                    core_in.at[l, yy], y_in.at[l, d - 1],
                    y_s.at[l, d - 1], y_r.at[l, d - 1], y_ids[d - 1],
                )
                copy.start()
                y_copies[l].append(copy)

    @pl.when(zh == 1)
    def _():
        fars[1].start()

    @pl.when(zh == 0)
    def _():
        code_blocks(0)
        for copy in away_copies:
            copy.start()

    code_blocks(1)
    for copy in own_copies:
        copy.start()

    @pl.when(zh == 1)
    def _():
        fars[2].start()


    def needed(at):
        return (at // 2, 2 - at % 2 + at // 2, 3 + at // 2)

    z1_copies = [[] for _ in range(CUTS)]
    for l in range(CUTS):
        for copy in y_copies[l]:
            copy.wait_recv()
        total = core_in[l, y] + y_in[l, 0] + y_in[l, 1] + y_in[l, 2]
        total = total.reshape(5, 16, wide)
        for at in range(4):
            for s, group in enumerate(needed(at)):
                classes[l, at, s] = total[group]
        for d in (1, 2, 3):
            copy = remote(
                classes.at[l, (b + d) % 4], z1_in.at[l, d - 1],
                z1_s.at[l, d - 1], z1_r.at[l, d - 1], quad_ids[d - 1],
            )
            copy.start()
            z1_copies[l].append(copy)

    @pl.when(zh == 1)
    def _():
        fars[3].start()

    d_own = diagonal([dec[mp * 5 + g] for g in range(5)]).astype(F32)
    dmain[...] = jnp.concatenate([d_own, d_own], axis=0).astype(BF16)
    dtail_a[...] = jnp.concatenate([d_own[0:40], d_own[0:40]], axis=0).astype(BF16)
    dtail_b[...] = jnp.concatenate([d_own[40:80], d_own[40:80]], axis=0).astype(BF16)

    w2_v = w2[...].reshape(640, 384)
    grad = dot(chi[...].reshape(640, 192), w2_v, TN)
    grad = grad + dot(clo[...].reshape(640, 192), w2_v, TN)
    gattn_out[...] = grad.astype(BF16)

    single = b % 2 == q
    z2a_copies = []
    for l in range(CUTS):
        for copy in z1_copies[l]:
            copy.wait_recv()
        quad[l] = classes[l, b] + z1_in[l, 0] + z1_in[l, 1] + z1_in[l, 2]
        two = remote(
            quad.at[l, pl.ds(1 - q, 2)], z2a_in.at[l], z2a_s.at[l], z2a_r.at[l], z4_id
        )
        one = remote(
            quad.at[l, pl.ds(2 - 2 * q, 1)], z2a_in.at[l, pl.ds(1 - q, 1)],
            z2a_s.at[l], z2a_r.at[l], z4_id,
        )
        z2a_copies.append((one, two))

        @pl.when(single)
        def _(two=two):
            two.start()

        @pl.when(jnp.logical_not(single))
        def _(one=one):
            one.start()

    for copy in own_copies:
        copy.wait_recv()
    code_near = blk[1, x] + x_in[1, 0] + x_in[1, 1] + x_in[1, 2]

    @pl.when(half == 0)
    def _():
        pl.semaphore_wait(ready8, 1)

    z2b_copies = [
        (
            remote(
                pair.at[l, pl.ds(q, 1)], z2b_in.at[l, pl.ds(q, 1)],
                z2b_s.at[l], z2b_r.at[l], z8_id,
            ),
            remote(pair.at[l], z2b_in.at[l], z2b_s.at[l], z2b_r.at[l], z8_id),
        )
        for l in range(CUTS)
    ]
    fin_copies = [
        remote(whole.at[l], whole.at[l], fin_s.at[l], fin_r.at[l], other_core) for l in range(CUTS)
    ]
    for l in range(CUTS):
        pair[l] = quad[l, pl.ds(q, 2)]

        @pl.when(single)
        def _(l=l):
            z2a_copies[l][0].wait_recv()
            pair[l, q] = pair[l, q] + z2a_in[l, q]

            @pl.when(half != core)
            def _():
                z2b_copies[l][0].start()

        @pl.when(jnp.logical_not(single))
        def _(l=l):
            z2a_copies[l][1].wait_recv()
            pair[l] = pair[l] + z2a_in[l]

            @pl.when(half != core)
            def _():
                z2b_copies[l][1].start()

    @pl.when(zh == 0)
    def _():
        pl.semaphore_wait(ready16, 1)
        send_away()
        for copy in fars[1:]:
            copy.start()

    for copy in fars:
        copy.wait_recv()
    last.start()

    @pl.when(half == core)
    def _():
        for l in range(CUTS):
            whole[l] = pair[l]

            @pl.when(single)
            def _(l=l):
                z2b_copies[l][0].wait_recv()
                whole[l, q] = whole[l, q] + z2b_in[l, q]

            @pl.when(jnp.logical_not(single))
            def _(l=l):
                z2b_copies[l][1].wait_recv()
                whole[l] = whole[l] + z2b_in[l]

            fin_copies[l].start()

    last.wait_recv()
    code_sum = code_near + far_in[...]
    high, low = split(code_sum)
    main = jnp.concatenate([high[0:80], low[0:80]], axis=0).astype(BF16)
    tail = jnp.concatenate([high[80:120], low[80:120]], axis=0).astype(BF16)
    mixed_out[0:128, :] = dot(main, dmain[...], TN).astype(BF16)
    tail_a = dot(tail, dtail_a[...], TN)
    tail_b = dot(tail, dtail_b[...], TN)
    mixed_out[128:192, :] = (tail_a[0:64] + tail_b[64:128]).astype(BF16)

    groups = needed(b)
    first = groups[0] * (1 - q) + groups[1] * q
    second = groups[1] * (1 - q) + groups[2] * q
    base = (2 * y + half) * 5
    e_pair = diagonal([enc[base + first], enc[base + second]])
    e_both = jnp.concatenate([e_pair, e_pair], axis=0)

    @pl.when(half != core)
    def _():
        for l in range(CUTS):
            fin_copies[l].wait_recv()

    for l in range(CUTS):
        g_high, g_low = split(whole[l].reshape(32, wide))
        g_both = jnp.concatenate([g_high, g_low], axis=0).astype(BF16)
        gw_rows[:, wide * l:wide * (l + 1)] = dot(e_both, g_both, TN) * scale
    jump = (b % 2) * q
    start = 40 * (2 * j + core) - 128 * (first * (1 - jump) + (second - 1) * jump)
    gw_out[...] = gw_rows[pl.ds(pl.multiple_of(start, 8), 40), :]

    for copy in core_copies + away_copies + own_copies + fars + [last]:
        copy.wait_send()
    for l in range(CUTS):
        for copy in y_copies[l] + z1_copies[l]:
            copy.wait_send()

    for pick, want in ((0, single), (1, jnp.logical_not(single))):
        @pl.when(want)
        def _(pick=pick):
            for l in range(CUTS):
                z2a_copies[l][1 - pick].wait_send()

                @pl.when(half != core)
                def _(l=l):
                    z2b_copies[l][pick].wait_send()

    @pl.when(half == core)
    def _():
        for l in range(CUTS):
            fin_copies[l].wait_send()


def finish(mixed, gattn, gw, mixed_out, gattn_out, gw_out, sem):
    copies = [
        pltpu.make_async_copy(mixed, mixed_out, sem.at[0]),
        pltpu.make_async_copy(gattn, gattn_out, sem.at[1]),
        pltpu.make_async_copy(gw, gw_out, sem.at[2]),
    ]
    for copy in copies:
        copy.start()
    for copy in copies:
        copy.wait()


def solution(mesh):
    dp_count = mesh.shape["dp"]

    def shards(attn, w_out, encoder, decoder, cotangent):
        scale = float(attn.shape[0] * dp_count) ** (-0.5)
        enc_t = jnp.transpose(encoder, (0, 2, 1))
        wide = 384 // CUTS
        hbm = pl.BlockSpec(memory_space=pltpu.HBM)
        near = pl.BlockSpec(memory_space=pltpu.VMEM)
        shapes = (
            jax.ShapeDtypeStruct((192, 640), BF16),
            jax.ShapeDtypeStruct((192, 384), BF16),
            jax.ShapeDtypeStruct((40, 384), F32),
        )
        dma = pltpu.SemaphoreType.DMA
        vmem = pltpu.VMEM
        results = pl.pallas_call(
            functools.partial(kernel, scale),
            out_shape=shapes,
            in_specs=[hbm] * 5,
            out_specs=(near,) * 3,
            scratch_shapes=[
                vmem((192, 384), BF16),
                vmem((8, 640, 384), BF16),
                vmem((40, 16, 128), BF16),
                vmem((40, 16, 128), BF16),
                vmem((8, 192, 640), BF16),
                vmem((8, 80, 384), BF16),
                vmem((8, 80, 192), BF16),
                vmem((8, 80, 192), BF16),
                vmem((CUTS, 2, 4, 80, wide), F32),
                vmem((CUTS, 4, 80, wide), F32),
                vmem((CUTS, 3, 80, wide), F32),
                vmem((CUTS, 4, 3, 16, wide), F32),
                vmem((CUTS, 3, 3, 16, wide), F32),
                vmem((CUTS, 3, 16, wide), F32),
                vmem((CUTS, 2, 16, wide), F32),
                vmem((CUTS, 2, 16, wide), F32),
                vmem((CUTS, 2, 16, wide), F32),
                vmem((CUTS, 2, 16, wide), F32),
                vmem((2, 4, 120, 128), F32),
                vmem((2, 3, 120, 128), F32),
                vmem((120, 128), F32),
                vmem((120, 128), F32),
                vmem((120, 128), F32),
                vmem((160, 640), BF16),
                vmem((80, 640), BF16),
                vmem((80, 640), BF16),
                vmem((256, 384), F32),
                dma((3,)), dma((8,)), dma((8,)),
                pltpu.SemaphoreType.REGULAR, pltpu.SemaphoreType.REGULAR,
                dma((3,)), dma((3,)),
                dma((3, 3)), dma((3, 3)),
                dma((2, 3)), dma((2, 3)),
                dma((3, 3)), dma((3, 3)),
                dma((3,)), dma((3,)),
                dma((3,)), dma((3,)),
                dma((3,)), dma((3,)),
                dma((4,)), dma((4,)),
                dma, dma,
            ],
            compiler_params=pltpu.CompilerParams(
                collective_id=0, has_side_effects=True, vmem_limit_bytes=56 * 1024 * 1024
            ),
            name="coded_projection",
        )(attn, w_out, enc_t, decoder, cotangent)
        return pl.pallas_call(
            finish,
            out_shape=shapes,
            in_specs=[near] * 3,
            out_specs=(hbm,) * 3,
            scratch_shapes=[dma((3,))],
            name="finish",
        )(*results)

    return jax.shard_map(
        shards,
        mesh=mesh,
        in_specs=(P("dp", "mp"), P(None, "mp"), P(), P(), P("dp", None)),
        out_specs=(P("dp", "mp"), P("dp", "mp"), P("dp", "mp")),
        check_vma=False,
    )
```

```python
import functools

import jax
import jax.numpy as jnp
from jax import lax
from jax.experimental import pallas as pl
from jax.experimental.pallas import tpu as pltpu
from jax.sharding import PartitionSpec as P

MESH = pl.DeviceIdType.MESH
CUTS = 3
F32 = jnp.float32
BF16 = jnp.bfloat16
NN = (((1,), (0,)), ((), ()))
NT = (((1,), (1,)), ((), ()))
TN = (((0,), (0,)), ((), ()))


def dot(a, b, dims):
    return lax.dot_general(a, b, dims, preferred_element_type=F32)


def diagonal(blocks):
    zero = jnp.zeros_like(blocks[0])
    rows = [
        jnp.concatenate([b if i == j else zero for j in range(len(blocks))], axis=1)
        for i, b in enumerate(blocks)
    ]
    return jnp.concatenate(rows, axis=0)


def split(value):
    high = value.astype(BF16).astype(F32)
    return high, value - high


def kernel(
    scale,
    attn_hbm, w_hbm, enc_hbm, dec_hbm, cot_hbm,
    mixed_out, gattn_out, gw_out,
    attn, w, enc, dec, cot,
    w2, chi, clo, term, core_in, y_in, classes, z1_in, quad, z2a_in, z2b_in, pair, whole,
    blk, x_in, zsum, relay_in, far_in, dmain, dtail_a, dtail_b, gw_rows,
    in_sem, w_sem, cot_sem, ready8, ready16,
    core_s, core_r, y_s, y_r, x_s, x_r, z1_s, z1_r, z2a_s, z2a_r, z2b_s, z2b_r,
    fin_s, fin_r, far_s, far_r, rel_s, rel_r,
):
    dp = lax.axis_index("dp")
    mp = lax.axis_index("mp")
    core = dp % 2
    zl = (dp // 2) % 16
    y = dp // 32
    x = mp // 2
    zh = mp % 2
    a = zl // 4
    b = zl % 4
    q = a % 2
    half = a // 2
    j = zl % 8

    other_core = (dp + 1 - 2 * core, mp)
    x_ids = [(dp, ((x + d) % 4) * 2 + zh) for d in (1, 2, 3)]
    y_ids = [((((y + d) % 4) * 16 + zl) * 2 + core, mp) for d in (1, 2, 3)]
    quad_ids = [((y * 16 + a * 4 + (b + d) % 4) * 2 + core, mp) for d in (1, 2, 3)]
    z4_id = ((y * 16 + zl + 4 - 8 * q) * 2 + core, mp)
    z8_id = ((y * 16 + zl + 8 - 16 * half) * 2 + core, mp)

    def remote(src, dst, send, recv, to):
        return pltpu.make_async_remote_copy(
            src_ref=src, dst_ref=dst, send_sem=send, recv_sem=recv,
            device_id=to, device_id_type=MESH,
        )

    barrier = pltpu.get_barrier_semaphore()
    near = [other_core] + x_ids + y_ids + quad_ids + [z4_id]
    z16_id = ((y * 16 + a * 4 + (b + 2) % 4) * 2 + core, x * 2 + 1 - zh)
    for to in near:
        pl.semaphore_signal(barrier, inc=1, device_id=to, device_id_type=MESH)

    @pl.when(half == 0)
    def _():
        pl.semaphore_signal(barrier, inc=1, device_id=z8_id, device_id_type=MESH)

    @pl.when(zh == 0)
    def _():
        pl.semaphore_signal(barrier, inc=1, device_id=z16_id, device_id_type=MESH)

    attn_copy = pltpu.make_async_copy(attn_hbm, attn, in_sem.at[0])
    dec_copy = pltpu.make_async_copy(dec_hbm, dec, in_sem.at[1])
    enc_copy = pltpu.make_async_copy(enc_hbm, enc, in_sem.at[2])
    dec_copy.start()
    attn_copy.start()
    cot_order = [2 * i + 1 - core for i in range(4)] + [2 * i + core for i in range(4)]
    cot_copies = []
    for i, m in enumerate(cot_order):
        cols = pl.ds(pl.multiple_of(m * 640, 128), 640)
        cot_copies.append(pltpu.make_async_copy(cot_hbm.at[:, cols], cot.at[i], cot_sem.at[i]))
    w_order = [(((x + d) % 4) * 2 + 1 - zh) for d in (1, 2, 3, 0)]
    w_order += [(((x + d) % 4) * 2 + zh) for d in (1, 2, 3, 0)]
    w_copies = []
    for i, m in enumerate(w_order):
        rows = pl.ds(pl.multiple_of(m * 640, 128), 640)
        w_copies.append(pltpu.make_async_copy(w_hbm.at[rows, :], w.at[i], w_sem.at[i]))

    enc_copy.start()

    @pl.when(zh == 0)
    def _():
        for copy in cot_copies + w_copies:
            copy.start()

    @pl.when(zh == 1)
    def _():
        for copy in w_copies[:4] + cot_copies + w_copies[4:]:
            copy.start()

    dec_copy.wait()
    attn_copy.wait()

    wide = 384 // CUTS

    def gradient_terms(side):
        for i in range(4):
            cot_copies[4 * side + i].wait()
        for i in range(4 * side, 4 * side + 4):
            m = cot_order[i]
            d_block = diagonal([dec[m * 5 + g] for g in range(5)])
            coded = dot(d_block, cot[i], NT)
            high, low = split(coded)
            high = high.astype(BF16)
            chi[m] = high
            clo[m] = low.astype(BF16)
            product = dot(high, attn[...], NN)
            for l in range(CUTS):
                term[l, m % 2, m // 2] = product[:, wide * l:wide * (l + 1)]

    def code_blocks(side):
        for i in range(4):
            w_copies[4 * side + i].wait()
        for i in range(4):
            m = w_order[4 * side + i]
            to = m // 2
            e_block = diagonal([enc[m * 5 + g] for g in range(5)])
            w2_block = dot(e_block, w[4 * side + i], NN).astype(BF16)
            w2[m] = w2_block
            code = dot(w2_block, attn[...], NT)
            blk[side, to, 0:80, :] = code[:, 0:128]
            blk[side, to, 80:120, :] = jnp.concatenate(
                [code[0:40, 128:192], code[40:80, 128:192]], axis=1
            )

    away_copies, own_copies = [
        [
            remote(
                blk.at[side, (x + d) % 4], x_in.at[side, d - 1],
                x_s.at[side, d - 1], x_r.at[side, d - 1], x_ids[d - 1],
            )
            for d in (1, 2, 3)
        ]
        for side in (0, 1)
    ]

    enc_copy.wait()

    @pl.when(zh == 0)
    def _():
        gradient_terms(0)

    @pl.when(zh == 1)
    def _():
        code_blocks(0)

    pl.semaphore_wait(barrier, len(near) + half + zh)

    @pl.when(zh == 1)
    def _():
        for copy in away_copies:
            copy.start()
        gradient_terms(0)

    core_copies = []
    for l in range(CUTS):
        copy = remote(
            term.at[l, 1 - core], core_in.at[l], core_s.at[l], core_r.at[l], other_core
        )
        copy.start()
        core_copies.append(copy)

    @pl.when(half == 1)
    def _():
        pl.semaphore_signal(ready8, inc=1, device_id=z8_id, device_id_type=MESH)

    @pl.when(zh == 1)
    def _():
        pl.semaphore_signal(ready16, inc=1, device_id=z16_id, device_id_type=MESH)

    gradient_terms(1)

    pieces = [pl.ds(0, 32), pl.ds(32, 32), pl.ds(64, 32), pl.ds(96, 24)]
    fars = [
        remote(zsum.at[piece], relay_in.at[piece], far_s.at[i], far_r.at[i], z16_id)
        for i, piece in enumerate(pieces)
    ]
    last = remote(relay_in, far_in, rel_s, rel_r, quad_ids[1])

    def send_away():
        for copy in away_copies:
            copy.wait_recv()
        zsum[...] = blk[0, x] + x_in[0, 0] + x_in[0, 1] + x_in[0, 2]

    @pl.when(zh == 1)
    def _():
        send_away()

    y_copies = [[] for _ in range(CUTS)]
    for l in range(CUTS):
        core_copies[l].wait_recv()
        for d in (1, 2, 3, 0):
            yy = (y + d) % 4
            core_in[l, yy] = core_in[l, yy] + term[l, core, yy]
            if d:
                copy = remote(
                    core_in.at[l, yy], y_in.at[l, d - 1],
                    y_s.at[l, d - 1], y_r.at[l, d - 1], y_ids[d - 1],
                )
                copy.start()
                y_copies[l].append(copy)

    @pl.when(zh == 1)
    def _():
        fars[0].start()

    @pl.when(zh == 0)
    def _():
        code_blocks(0)
        for copy in away_copies:
            copy.start()

    code_blocks(1)
    for copy in own_copies:
        copy.start()

    @pl.when(zh == 1)
    def _():
        fars[1].start()


    def needed(at):
        return (at // 2, 2 - at % 2 + at // 2, 3 + at // 2)

    z1_copies = [[] for _ in range(CUTS)]
    for l in range(CUTS):
        for copy in y_copies[l]:
            copy.wait_recv()
        total = core_in[l, y] + y_in[l, 0] + y_in[l, 1] + y_in[l, 2]
        total = total.reshape(5, 16, wide)
        for at in range(4):
            for s, group in enumerate(needed(at)):
                classes[l, at, s] = total[group]
        for d in (1, 2, 3):
            copy = remote(
                classes.at[l, (b + d) % 4], z1_in.at[l, d - 1],
                z1_s.at[l, d - 1], z1_r.at[l, d - 1], quad_ids[d - 1],
            )
            copy.start()
            z1_copies[l].append(copy)

    @pl.when(zh == 1)
    def _():
        fars[2].start()

    d_own = diagonal([dec[mp * 5 + g] for g in range(5)]).astype(F32)
    dmain[...] = jnp.concatenate([d_own, d_own], axis=0).astype(BF16)
    dtail_a[...] = jnp.concatenate([d_own[0:40], d_own[0:40]], axis=0).astype(BF16)
    dtail_b[...] = jnp.concatenate([d_own[40:80], d_own[40:80]], axis=0).astype(BF16)

    w2_v = w2[...].reshape(640, 384)
    grad = dot(chi[...].reshape(640, 192), w2_v, TN)
    grad = grad + dot(clo[...].reshape(640, 192), w2_v, TN)
    gattn_out[...] = grad.astype(BF16)

    @pl.when(zh == 1)
    def _():
        fars[3].start()

    single = b % 2 == q
    z2a_copies = []
    for l in range(CUTS):
        for copy in z1_copies[l]:
            copy.wait_recv()
        quad[l] = classes[l, b] + z1_in[l, 0] + z1_in[l, 1] + z1_in[l, 2]
        two = remote(
            quad.at[l, pl.ds(1 - q, 2)], z2a_in.at[l], z2a_s.at[l], z2a_r.at[l], z4_id
        )
        one = remote(
            quad.at[l, pl.ds(2 - 2 * q, 1)], z2a_in.at[l, pl.ds(1 - q, 1)],
            z2a_s.at[l], z2a_r.at[l], z4_id,
        )
        z2a_copies.append((one, two))

        @pl.when(single)
        def _(two=two):
            two.start()

        @pl.when(jnp.logical_not(single))
        def _(one=one):
            one.start()

    for copy in own_copies:
        copy.wait_recv()
    code_near = blk[1, x] + x_in[1, 0] + x_in[1, 1] + x_in[1, 2]

    @pl.when(half == 0)
    def _():
        pl.semaphore_wait(ready8, 1)

    z2b_copies = [
        (
            remote(
                pair.at[l, pl.ds(q, 1)], z2b_in.at[l, pl.ds(q, 1)],
                z2b_s.at[l], z2b_r.at[l], z8_id,
            ),
            remote(pair.at[l], z2b_in.at[l], z2b_s.at[l], z2b_r.at[l], z8_id),
        )
        for l in range(CUTS)
    ]
    fin_copies = [
        remote(whole.at[l], whole.at[l], fin_s.at[l], fin_r.at[l], other_core) for l in range(CUTS)
    ]
    for l in range(CUTS):
        pair[l] = quad[l, pl.ds(q, 2)]

        @pl.when(single)
        def _(l=l):
            z2a_copies[l][0].wait_recv()
            pair[l, q] = pair[l, q] + z2a_in[l, q]

            @pl.when(half != core)
            def _():
                z2b_copies[l][0].start()

        @pl.when(jnp.logical_not(single))
        def _(l=l):
            z2a_copies[l][1].wait_recv()
            pair[l] = pair[l] + z2a_in[l]

            @pl.when(half != core)
            def _():
                z2b_copies[l][1].start()

    @pl.when(zh == 0)
    def _():
        pl.semaphore_wait(ready16, 1)
        send_away()
        for copy in fars:
            copy.start()

    for copy in fars:
        copy.wait_recv()
    last.start()

    @pl.when(half == core)
    def _():
        for l in range(CUTS):
            whole[l] = pair[l]

            @pl.when(single)
            def _(l=l):
                z2b_copies[l][0].wait_recv()
                whole[l, q] = whole[l, q] + z2b_in[l, q]

            @pl.when(jnp.logical_not(single))
            def _(l=l):
                z2b_copies[l][1].wait_recv()
                whole[l] = whole[l] + z2b_in[l]

            fin_copies[l].start()

    last.wait_recv()
    code_sum = code_near + far_in[...]
    high, low = split(code_sum)
    main = jnp.concatenate([high[0:80], low[0:80]], axis=0).astype(BF16)
    tail = jnp.concatenate([high[80:120], low[80:120]], axis=0).astype(BF16)
    mixed_out[0:128, :] = dot(main, dmain[...], TN).astype(BF16)
    tail_a = dot(tail, dtail_a[...], TN)
    tail_b = dot(tail, dtail_b[...], TN)
    mixed_out[128:192, :] = (tail_a[0:64] + tail_b[64:128]).astype(BF16)

    groups = needed(b)
    first = groups[0] * (1 - q) + groups[1] * q
    second = groups[1] * (1 - q) + groups[2] * q
    base = (2 * y + half) * 5
    e_pair = diagonal([enc[base + first], enc[base + second]])
    e_both = jnp.concatenate([e_pair, e_pair], axis=0)

    @pl.when(half != core)
    def _():
        for l in range(CUTS):
            fin_copies[l].wait_recv()

    for l in range(CUTS):
        g_high, g_low = split(whole[l].reshape(32, wide))
        g_both = jnp.concatenate([g_high, g_low], axis=0).astype(BF16)
        gw_rows[:, wide * l:wide * (l + 1)] = dot(e_both, g_both, TN) * scale
    jump = (b % 2) * q
    start = 40 * (2 * j + core) - 128 * (first * (1 - jump) + (second - 1) * jump)
    gw_out[...] = gw_rows[pl.ds(pl.multiple_of(start, 8), 40), :]

    for copy in core_copies + away_copies + own_copies + fars + [last]:
        copy.wait_send()
    for l in range(CUTS):
        for copy in y_copies[l] + z1_copies[l]:
            copy.wait_send()

    for pick, want in ((0, single), (1, jnp.logical_not(single))):
        @pl.when(want)
        def _(pick=pick):
            for l in range(CUTS):
                z2a_copies[l][1 - pick].wait_send()

                @pl.when(half != core)
                def _(l=l):
                    z2b_copies[l][pick].wait_send()

    @pl.when(half == core)
    def _():
        for l in range(CUTS):
            fin_copies[l].wait_send()


def finish(mixed, gattn, gw, mixed_out, gattn_out, gw_out, sem):
    copies = [
        pltpu.make_async_copy(mixed, mixed_out, sem.at[0]),
        pltpu.make_async_copy(gattn, gattn_out, sem.at[1]),
        pltpu.make_async_copy(gw, gw_out, sem.at[2]),
    ]
    for copy in copies:
        copy.start()
    for copy in copies:
        copy.wait()


def solution(mesh):
    dp_count = mesh.shape["dp"]

    def shards(attn, w_out, encoder, decoder, cotangent):
        scale = float(attn.shape[0] * dp_count) ** (-0.5)
        enc_t = jnp.transpose(encoder, (0, 2, 1))
        wide = 384 // CUTS
        hbm = pl.BlockSpec(memory_space=pltpu.HBM)
        near = pl.BlockSpec(memory_space=pltpu.VMEM)
        shapes = (
            jax.ShapeDtypeStruct((192, 640), BF16),
            jax.ShapeDtypeStruct((192, 384), BF16),
            jax.ShapeDtypeStruct((40, 384), F32),
        )
        dma = pltpu.SemaphoreType.DMA
        vmem = pltpu.VMEM
        results = pl.pallas_call(
            functools.partial(kernel, scale),
            out_shape=shapes,
            in_specs=[hbm] * 5,
            out_specs=(near,) * 3,
            scratch_shapes=[
                vmem((192, 384), BF16),
                vmem((8, 640, 384), BF16),
                vmem((40, 16, 128), BF16),
                vmem((40, 16, 128), BF16),
                vmem((8, 192, 640), BF16),
                vmem((8, 80, 384), BF16),
                vmem((8, 80, 192), BF16),
                vmem((8, 80, 192), BF16),
                vmem((CUTS, 2, 4, 80, wide), F32),
                vmem((CUTS, 4, 80, wide), F32),
                vmem((CUTS, 3, 80, wide), F32),
                vmem((CUTS, 4, 3, 16, wide), F32),
                vmem((CUTS, 3, 3, 16, wide), F32),
                vmem((CUTS, 3, 16, wide), F32),
                vmem((CUTS, 2, 16, wide), F32),
                vmem((CUTS, 2, 16, wide), F32),
                vmem((CUTS, 2, 16, wide), F32),
                vmem((CUTS, 2, 16, wide), F32),
                vmem((2, 4, 120, 128), F32),
                vmem((2, 3, 120, 128), F32),
                vmem((120, 128), F32),
                vmem((120, 128), F32),
                vmem((120, 128), F32),
                vmem((160, 640), BF16),
                vmem((80, 640), BF16),
                vmem((80, 640), BF16),
                vmem((256, 384), F32),
                dma((3,)), dma((8,)), dma((8,)),
                pltpu.SemaphoreType.REGULAR, pltpu.SemaphoreType.REGULAR,
                dma((3,)), dma((3,)),
                dma((3, 3)), dma((3, 3)),
                dma((2, 3)), dma((2, 3)),
                dma((3, 3)), dma((3, 3)),
                dma((3,)), dma((3,)),
                dma((3,)), dma((3,)),
                dma((3,)), dma((3,)),
                dma((4,)), dma((4,)),
                dma, dma,
            ],
            compiler_params=pltpu.CompilerParams(
                collective_id=0, has_side_effects=True, vmem_limit_bytes=56 * 1024 * 1024
            ),
            name="coded_projection",
        )(attn, w_out, enc_t, decoder, cotangent)
        return pl.pallas_call(
            finish,
            out_shape=shapes,
            in_specs=[near] * 3,
            out_specs=(hbm,) * 3,
            scratch_shapes=[dma((3,))],
            name="finish",
        )(*results)

    return jax.shard_map(
        shards,
        mesh=mesh,
        in_specs=(P("dp", "mp"), P(None, "mp"), P(), P(), P("dp", None)),
        out_specs=(P("dp", "mp"), P("dp", "mp"), P("dp", "mp")),
        check_vma=False,
    )
```
